512 devices in a mesh: dp: 16 (over y, z_hi), pipe: 4 (over x), mp: 8 (over z_lo, core).
Axes of the slice: x: 4, y: 4, z: 16 (z_hi: 4, z_lo: 4; z = z_hi * 4 + z_lo), core: 2. Of those that a mesh axis runs over, the one named last changes fastest.
Arguments:
- enc_out: bfloat16 [4096, 4096], P(('dp', 'pipe'), 'mp'), may hold values from -6 to 6
- query: bfloat16 [4, 4096, 4096], P('pipe', 'dp', 'mp'), may hold values from -96 to 96
- w_key: bfloat16 [4, 4096, 4096], P('pipe', 'dp', 'mp'), may hold values from -0.09375 to 0.09375
- w_value: bfloat16 [4, 4096, 4096], P('pipe', 'dp', 'mp'), may hold values from -0.09375 to 0.09375
- d_context: bfloat16 [4, 4096, 4096], P('pipe', 'dp', 'mp'), may hold values from -6 to 6
- enc_lengths: int32 [16], P('dp'), may hold values from 32 to 256
- dec_lengths: int32 [16], P('dp'), may hold values from 32 to 256
Outputs:
- context: bfloat16 [4, 4096, 4096], P('pipe', 'dp', 'mp')
- grad_query: bfloat16 [4, 4096, 4096], P('pipe', 'dp', 'mp')
- grad_enc: float32 [4096, 4096], P(('dp', 'pipe'), 'mp')
The draws below stay inside these ranges and needn't reach their ends.
All inputs are finite; a program needn't handle non-finite values.
Results may differ from the reference program's by a relative error of at most 0.024.
The reference program's roundings to bfloat16 on the way (of `key_rows`, `value_rows`, `rounded`, `masked`, `grad_scores`, `grad_key` and `grad_value`) count: a program that leaves them out, or rounds other values in their place, can miss the bound.
Values may be sent and summed in bfloat16 or wider, within the bound.
A program may use at most 64 MiB of HBM per device.

```python
import jax
import jax.numpy as jnp
from jax import lax

D = 4096
HEADS = 16
HD = 256
ENC_LEN = 256
DEC_LEN = 256
SECTIONS = 4
REPLICAS = 16


def draw_query(key, part):
    key = jax.random.fold_in(key, 11)
    base_key = jax.random.fold_in(key, 0)
    shape = (SECTIONS, REPLICAS * DEC_LEN, HEADS * HD)
    base = jnp.clip(jax.random.normal(base_key, shape, jnp.float32), -6.0, 6.0)
    return base.astype(jnp.bfloat16)


def touch_ends(result, key, low, high):
    dims = result.shape
    place = [jax.random.randint(jax.random.fold_in(key, axis), (), 0, dims[axis]) for axis in range(len(dims))]
    result = result.at[tuple(place)].set(low)
    longest = dims.index(max(dims))
    place[longest] = (place[longest] + 1) % dims[longest]
    return result.at[tuple(place)].set(high)


def steps_of(rng, shape, pieces, smallest, high):
    def one(axis_at, blocks):
        heights = jax.random.uniform(jax.random.fold_in(jax.random.fold_in(rng, 6), axis_at), (blocks,), jnp.float32, smallest / len(pieces), high / len(pieces))
        return jnp.repeat(jnp.exp(heights), shape[axis_at] // blocks).reshape((-1,) + (1,) * (len(shape) - axis_at - 1))

    gain = one(*pieces[0])
    for cut in pieces[1:]:
        gain = gain * one(*cut)
    return gain


def gaussian(key, dims, deviation, most, pieces=(), kind=jnp.bfloat16):
    values = deviation * jax.random.normal(key, dims, jnp.float32)
    if pieces:
        values = values * steps_of(key, dims, pieces, -0.22, 0.18)
    return jnp.clip(values, -most, most).astype(kind)


def setup_inputs(seed: int = 0) -> dict:
    streams_of = jax.random.split(jax.random.key(seed), 8)
    enc_out = gaussian(streams_of[0], (REPLICAS * ENC_LEN, D), 1.0, 6.0, ((0, 64), (1, 8)))
    query = draw_query(jax.random.fold_in(streams_of[7], 71), 0)
    w_key = gaussian(streams_of[2], (SECTIONS, D, HEADS * HD), D ** -0.5, 0.09375, ((0, 4), (1, 16), (2, 8)))
    w_value = gaussian(streams_of[3], (SECTIONS, D, HEADS * HD), D ** -0.5, 0.09375, ((0, 4), (1, 16), (2, 8)))
    d_context = gaussian(streams_of[4], (SECTIONS, REPLICAS * DEC_LEN, HEADS * HD), 1.0, 6.0, ((0, 4), (1, 16), (2, 8)))
    enc_lengths = touch_ends(jax.random.randint(streams_of[5], (REPLICAS,), ENC_LEN // 8, ENC_LEN + 1), jax.random.fold_in(streams_of[5], 1), ENC_LEN // 8, ENC_LEN).astype(jnp.int32)
    dec_lengths = touch_ends(jax.random.randint(streams_of[6], (REPLICAS,), DEC_LEN // 8, DEC_LEN + 1), jax.random.fold_in(streams_of[6], 1), DEC_LEN // 8, DEC_LEN).astype(jnp.int32)
    return dict(enc_out=enc_out, query=query, w_key=w_key, w_value=w_value, d_context=d_context, enc_lengths=enc_lengths, dec_lengths=dec_lengths)


NEG = -1e30


def attend(queries, key_rows, value_rows, cotangent, enc_length, dec_length):
    rows = queries.shape[0]
    length = key_rows.shape[0]
    heads = queries.shape[1] // HD
    scale = HD ** -0.5
    query_heads = queries.reshape(rows, heads, HD).astype(jnp.float32)
    key_heads = key_rows.reshape(length, heads, HD).astype(jnp.float32)
    value_heads = value_rows.reshape(length, heads, HD).astype(jnp.float32)
    scores = jnp.einsum("qhd,khd->hqk", query_heads, key_heads) * scale
    visible = jnp.arange(length, dtype=jnp.int32) < enc_length
    scores = jnp.where(visible[None, None, :], scores, NEG)
    row_max = jnp.max(scores, axis=2, keepdims=True)
    powers = jnp.exp(scores - row_max)
    attention = powers / jnp.sum(powers, axis=2, keepdims=True)
    rounded = lax.optimization_barrier(attention.astype(jnp.bfloat16)).astype(jnp.float32)
    context = jnp.einsum("hqk,khd->qhd", rounded, value_heads).reshape(rows, heads * HD).astype(jnp.bfloat16)
    live = (jnp.arange(rows, dtype=jnp.int32) < dec_length)[:, None]
    masked = jnp.where(live, cotangent, jnp.zeros_like(cotangent))
    masked_heads = masked.reshape(rows, heads, HD).astype(jnp.float32)
    grad_weights = jnp.einsum("qhd,khd->hqk", masked_heads, value_heads)
    context_heads = context.reshape(rows, heads, HD).astype(jnp.float32)
    row_inner = jnp.sum(masked_heads * context_heads, axis=2)
    grad_scores = attention * (grad_weights - row_inner.T[:, :, None]) * scale
    grad_scores = lax.optimization_barrier(grad_scores.astype(jnp.bfloat16)).astype(jnp.float32)
    grad_query = jnp.einsum("hqk,khd->qhd", grad_scores, key_heads).reshape(rows, heads * HD).astype(jnp.bfloat16)
    grad_key = jnp.einsum("hqk,qhd->khd", grad_scores, query_heads).reshape(length, heads * HD).astype(jnp.bfloat16)
    grad_value = jnp.einsum("hqk,qhd->khd", rounded, masked_heads).reshape(length, heads * HD).astype(jnp.bfloat16)
    return context, grad_query, grad_key, grad_value


def reference(enc_out, query, w_key, w_value, d_context, enc_lengths, dec_lengths):
    enc_blocks = enc_out.reshape(REPLICAS, ENC_LEN, D)
    width = query.shape[2]

    def regroup(array):
        return array.reshape(SECTIONS, REPLICAS, DEC_LEN, width).transpose(1, 0, 2, 3)

    def replica(items):
        enc_rows, queries, cotangents, enc_length, dec_length = items
        total = jnp.zeros((ENC_LEN, D), jnp.float32)
        contexts = []
        gradients = []
        for section in range(SECTIONS):
            key_rows = jnp.dot(enc_rows, w_key[section], preferred_element_type=jnp.float32).astype(jnp.bfloat16)
            value_rows = jnp.dot(enc_rows, w_value[section], preferred_element_type=jnp.float32).astype(jnp.bfloat16)
            context, grad_query, grad_key, grad_value = attend(queries[section], key_rows, value_rows, cotangents[section], enc_length, dec_length)
            total = total + jnp.dot(grad_key, w_key[section].T, preferred_element_type=jnp.float32)
            total = total + jnp.dot(grad_value, w_value[section].T, preferred_element_type=jnp.float32)
            contexts.append(context)
            gradients.append(grad_query)
        return jnp.stack(contexts), jnp.stack(gradients), total

    contexts, gradients, totals = lax.map(replica, (enc_blocks, regroup(query), regroup(d_context), enc_lengths, dec_lengths))

    def restore(array):
        return array.transpose(1, 0, 2, 3).reshape(SECTIONS, REPLICAS * DEC_LEN, width)

    return restore(contexts), restore(gradients), totals.reshape(REPLICAS * ENC_LEN, D)
```

```python
import jax
import jax.numpy as jnp
from jax import lax
from jax.experimental import pallas as pl
from jax.experimental.pallas import tpu as pltpu
from jax.sharding import PartitionSpec as P

HD = 256
NEG = -1e30
BF = jnp.bfloat16
F32 = jnp.float32
CUTS = 4
ROWS = 256 // CUTS
STEPS = 4 * CUTS

NT = (((1,), (1,)), ((), ()))
NN = (((1,), (0,)), ((), ()))
TN = (((0,), (0,)), ((), ()))


def dot(a, b, dims):
    return lax.dot_general(a, b, dims, preferred_element_type=F32)


def kernel(
    enc_len, dec_len, enc_ref, q_ref, wk_ref, wv_ref, dc_ref,
    ctx_ref, gq_ref, ge_ref,
    w, e, acc, kv, grads, s0, r0, part, x1s, x1r, x2s, x2r, zs, zr,
    ez_s, ez_r, ex_s, ex_r, ec_s, ec_r, z_s, z_r, y_s, y_r,
    c_s, c_r, x1_s, x1_r, x2_s, x2_r, q_s, q_r,
):
    dp, x, mp = lax.axis_index("dp"), lax.axis_index("pipe"), lax.axis_index("mp")
    y, zh = dp // 4, dp % 4
    zl, core = mp // 2, mp % 2
    up, down = ((y + 1) % 4) * 4 + zh, ((y + 3) % 4) * 4 + zh
    nxt, prv = y * 4 + (zh + 1) % 4, y * 4 + (zh + 3) % 4
    d_up, d_down = (up, x, mp), (down, x, mp)
    d_next, d_prev = (nxt, x, mp), (prv, x, mp)
    d_right, d_left = (dp, (x + 1) % 4, mp), (dp, (x + 3) % 4, mp)
    d_sib = (dp, x, zl * 2 + 1 - core)
    d_line = [(dp, x, ((zl + r) % 4) * 2 + core) for r in range(4)]

    def rc(src, dst, ssem, rsem, dev):
        return pltpu.make_async_remote_copy(
            src_ref=src, dst_ref=dst, send_sem=ssem, recv_sem=rsem,
            device_id=dev, device_id_type=pl.DeviceIdType.MESH,
        )

    barrier = pltpu.get_barrier_semaphore()
    partners = [d_up, d_down, d_next, d_prev, d_right, d_left, d_sib] + d_line[1:]
    for dev in partners:
        pl.semaphore_signal(barrier, inc=1, device_id=dev, device_id_type=pl.DeviceIdType.MESH)

    w[dp, 0] = wk_ref[0]
    w[dp, 1] = wv_ref[0]
    my_rows = pl.ds(pl.multiple_of(x * 64, 64), 64)
    e[2 * mp, my_rows, :] = enc_ref[:, :256]
    e[2 * mp + 1, my_rows, :] = enc_ref[:, 256:]
    pl.semaphore_wait(barrier, len(partners))

    def eblock(xx, zz, cc):
        return e.at[pl.ds(zz * 4 + cc * 2, 2), pl.ds(pl.multiple_of(xx * 64, 64), 64), :]

    def ehalf(xx, zz, cc, part_of):
        return e.at[zz * 4 + cc * 2 + part_of, pl.ds(pl.multiple_of(xx * 64, 64), 64), :]

    def e_line(r):
        b = eblock(x, zl, core)
        return rc(b, b, ez_s.at[r], ez_r.at[r], d_line[r])

    def e_line_in(r):
        b = eblock(x, (zl + 4 - r) % 4, core)
        return rc(b, b, ez_s.at[r], ez_r.at[r], d_line[r])

    for r in (2, 1, 3):
        e_line(r).start()

    def chunk(yy, zz, j, sub):
        start = pl.multiple_of(sub * ROWS, ROWS)
        return w.at[yy * 4 + zz, j, pl.ds(start, ROWS), :]

    def z_copy(t, forwarded, inbound):
        out = []
        for stream in (0, 1):
            if forwarded:
                j, sub = stream, t - 2 * CUTS
                away = 1 + inbound
            else:
                j = (t // CUTS + stream) % 2
                sub = t % CUTS
                away = inbound
            zz = (zh + 4 - away) % 4 if stream == 0 else (zh + away) % 4
            c = chunk(y, zz, j, sub)
            out.append(rc(c, c, z_s.at[stream, t], z_r.at[stream, t], d_next if stream == 0 else d_prev))
        return out

    def unit(i):
        p, sub = i // CUTS, i % CUTS
        kz = (zh + 3 * p + 3 * (p // 2) + 2 * (p // 3)) % 4
        vz = (zh + p + p // 2 + 2 * (p // 3)) % 4
        return (kz, vz), sub

    def y_direct(i, inbound):
        zz, sub = unit(i)
        out = []
        for j in (0, 1):
            for way in (0, 1):
                yy = y if not inbound else ((y + 3) % 4 if way == 0 else (y + 1) % 4)
                c = chunk(yy, zz[j], j, sub)
                n = j * 2 + way
                out.append(rc(c, c, y_s.at[n, i], y_r.at[n, i], d_up if way == 0 else d_down))
        return out

    def y_forward(i, inbound):
        zz, sub = unit(i)
        out = []
        for j in (0, 1):
            away = 1 + inbound
            yy = (y + 4 - away) % 4 if j == 0 else (y + away) % 4
            c = chunk(yy, zz[j], j, sub)
            out.append(rc(c, c, y_s.at[4 + j, i], y_r.at[4 + j, i], d_up if j == 0 else d_down))
        return out

    def start(copies):
        for c in copies:
            c.start()

    def received(copies):
        for c in copies:
            c.wait_recv()

    def sent(copies):
        for c in copies:
            c.wait_send()

    def loop(lo, hi, body):
        lax.fori_loop(lo, hi, lambda i, carry: (body(i), carry)[1], 0)

    def first(i):
        start(z_copy(i, False, 0))
        start(y_direct(i, 0))

    loop(0, CUTS, first)
    loop(CUTS, 2 * CUTS, lambda i: start(z_copy(i, False, 0)))

    def ex_direct(r, inbound):
        zz = (zl + 4 - r) % 4
        out = []
        for way in (0, 1):
            xx = x if not inbound else ((x + 3) % 4 if way == 0 else (x + 1) % 4)
            b = eblock(xx, zz, core)
            out.append(rc(b, b, ex_s.at[way, r], ex_r.at[way, r], d_right if way == 0 else d_left))
        return out

    def ex_forward(r, inbound):
        zz = (zl + 4 - r) % 4
        out = []
        for way in (0, 1):
            away = 1 + inbound
            xx = (x + 4 - away) % 4 if way == 0 else (x + away) % 4
            b = ehalf(xx, zz, core, way)
            out.append(rc(b, b, ex_s.at[2 + way, r], ex_r.at[2 + way, r], d_right if way == 0 else d_left))
        return out

    def ec_copy(r, inbound):
        cc = 1 - core if inbound else core
        b = e.at[pl.ds(((zl + 4 - r) % 4) * 4 + cc * 2, 2)]
        return rc(b, b, ec_s.at[r], ec_r.at[r], d_sib)

    start(ex_direct(0, 0))
    for r in (1, 3, 2):
        e_line_in(r).wait_recv()
        start(ex_direct(r, 0))
    for r in (0, 1, 3, 2):
        received(ex_direct(r, 1))
        start(ex_forward(r, 0))
    for r in (0, 1, 3, 2):
        received(ex_forward(r, 1))
        ec_copy(r, 0).start()

    def own_phase(i):
        received(y_direct(i, 1))
        start(y_forward(i, 0))

    loop(0, CUTS, own_phase)
    for r in (0, 1, 3, 2):
        ec_copy(r, 1).wait_recv()

    def add_block(yy, zz, begin=False):
        d = yy * 4 + zz
        rows = e[d]
        for j in (0, 1):
            term = dot(rows, w[d, j], NN)
            acc[j] = term if begin else acc[j] + term

    def z_last(i):
        t = i - CUTS
        received(z_copy(t, True, 1))
        start(y_direct(i, 0))
        received(y_direct(i - 1, 1))
        start(y_forward(i - 1, 0))
        received(y_forward(i - 2, 1))

    loop(0, CUTS, lambda i: received(y_forward(i, 1)))
    add_block(y, zh, True)
    loop(1, 4, lambda k: add_block((y + k) % 4, zh))

    def phase_one(i):
        t = i - CUTS
        received(z_copy(t, False, 1))
        start(z_copy(t + 2 * CUTS, True, 0))
        start(y_direct(i, 0))

        @pl.when(t >= 1)
        def _():
            received(y_direct(i - 1, 1))
            start(y_forward(i - 1, 0))

        @pl.when(t >= 2)
        def _():
            received(y_forward(i - 2, 1))

    def phase_two(i):
        received(z_copy(i - CUTS, False, 1))
        start(y_direct(i, 0))
        received(y_direct(i - 1, 1))
        start(y_forward(i - 1, 0))
        received(y_forward(i - 2, 1))

    loop(CUTS, 2 * CUTS, phase_one)
    loop(2 * CUTS, 3 * CUTS, phase_two)
    loop(3 * CUTS, 3 * CUTS + 2, z_last)

    def neighbours(k):
        add_block((y + k) % 4, (zh + 1) % 4)
        add_block((y + k) % 4, (zh + 3) % 4)

    loop(0, 4, neighbours)
    loop(3 * CUTS + 2, 4 * CUTS, z_last)
    received(y_direct(STEPS - 1, 1))
    start(y_forward(STEPS - 1, 0))
    received(y_forward(STEPS - 2, 1))
    far = (zh + 2) % 4
    add_block(y, far)
    add_block((y + 1) % 4, far)
    add_block((y + 3) % 4, far)
    received(y_forward(STEPS - 1, 1))
    add_block((y + 2) % 4, far)

    scale = HD ** -0.5
    kv[...] = acc[...].astype(BF)
    shape = (256, 256)
    visible = lax.broadcasted_iota(jnp.int32, shape, 1) < enc_len[0]
    live = lax.broadcasted_iota(jnp.int32, shape, 0) < dec_len[0]
    for h in (0, 1):
        cols = slice(h * HD, (h + 1) * HD)
        q = q_ref[0, :, cols]
        key, value = kv[0, :, cols], kv[1, :, cols]
        masked = jnp.where(live, dc_ref[0, :, cols].astype(F32), 0.0)
        masked16 = masked.astype(BF)
        scores = jnp.where(visible, dot(q, key, NT) * scale, NEG)
        powers = jnp.exp(scores - jnp.max(scores, axis=1, keepdims=True))
        attention = powers / jnp.sum(powers, axis=1, keepdims=True)
        rounded = attention.astype(BF)
        context = dot(rounded, value, NN).astype(BF)
        ctx_ref[0, :, cols] = context
        weights = dot(masked16, value, NT)
        inner = jnp.sum(masked * context.astype(F32), axis=1, keepdims=True)
        g = (attention * (weights - inner) * scale).astype(BF)
        gq_ref[0, :, cols] = dot(g, key, NN).astype(BF)
        grads[0, :, cols] = dot(g, q, TN).astype(BF)
        grads[1, :, cols] = dot(rounded, masked16, TN).astype(BF)

    def place(k):
        return (zl + 1 + k) % 4

    def enc_term(k, cc, half):
        d = place(k) * 4 + cc * 2 + half
        return dot(grads[0], w[d, 0], NT) + dot(grads[1], w[d, 1], NT)

    def c_copy(k):
        return rc(s0.at[k], r0.at[k], c_s.at[k], c_r.at[k], d_sib)

    def quarter(n):
        return pl.ds(pl.multiple_of(((x + n) % 4) * 64, 64), 64)

    def x1_copy(k):
        return [
            rc(x1s.at[k, way], x1r.at[k, way], x1_s.at[k, way], x1_r.at[k, way], dev)
            for way, dev in ((0, d_right), (1, d_left))
        ]

    def x2_copy(k):
        return [
            rc(x2s.at[k, way], x2r.at[k, way], x2_s.at[k, way], x2_r.at[k, way], dev)
            for way, dev in ((0, d_right), (1, d_left))
        ]

    def q_copy(k):
        return rc(zs.at[k], zr.at[k], q_s.at[k], q_r.at[k], d_line[k + 1])

    def to_sibling(k):
        for half in (0, 1):
            s0[k, half] = enc_term(k, 1 - core, half).astype(BF)
        c_copy(k).start()

    def mine(k):
        for half in (0, 1):
            part[k, half] = enc_term(k, core, half)
        c_copy(k).wait_recv()
        part[k] = part[k] + r0[k].astype(F32)
        for way in (0, 1):
            x1s[k, way] = part[k, way, quarter(2), :].astype(BF)
        start(x1_copy(k))

    def second(k):
        received(x1_copy(k))
        for way in (0, 1):
            away = quarter(1 + 2 * way)
            for half in (0, 1):
                term = part[k, half, away, :]
                if half == way:
                    term = term + x1r[k, way].astype(F32)
                x2s[k, way, half] = term.astype(BF)
        start(x2_copy(k))

    def third(k):
        received(x2_copy(k))
        total = part[k, :, quarter(0), :] + x2r[k, 0].astype(F32) + x2r[k, 1].astype(F32)
        part[k, :, quarter(0), :] = total

    loop(0, 4, to_sibling)
    loop(0, 4, mine)
    loop(0, 4, second)
    for k in range(3):
        third(k)
        zs[k] = part[k, :, quarter(0), :].astype(BF)
        q_copy(k).start()
    third(3)
    total = part[3, :, quarter(0), :]
    for k in range(3):
        q_copy(k).wait_recv()
        total = total + zr[k].astype(F32)
    ge_ref[:, :256] = total[0]
    ge_ref[:, 256:] = total[1]

    for r in range(1, 4):
        e_line(r).wait_send()
    for r in range(4):
        sent(ex_direct(r, 0))
        sent(ex_forward(r, 0))
        ec_copy(r, 0).wait_send()
    loop(0, 2 * CUTS, lambda t: sent(z_copy(t, False, 0)))
    loop(2 * CUTS, 3 * CUTS, lambda t: sent(z_copy(t, True, 0)))

    def y_sent(i):
        sent(y_direct(i, 0))
        sent(y_forward(i, 0))

    loop(0, STEPS, y_sent)

    def rest(k):
        c_copy(k).wait_send()
        sent(x1_copy(k))
        sent(x2_copy(k))

    loop(0, 4, rest)
    for k in range(3):
        q_copy(k).wait_send()


def body(enc_out, query, w_key, w_value, d_context, enc_lengths, dec_lengths):
    vmem = pl.BlockSpec(memory_space=pltpu.VMEM)
    smem = pl.BlockSpec(memory_space=pltpu.SMEM)
    dma = pltpu.SemaphoreType.DMA
    return pl.pallas_call(
        kernel,
        out_shape=(
            jax.ShapeDtypeStruct((1, 256, 512), BF),
            jax.ShapeDtypeStruct((1, 256, 512), BF),
            jax.ShapeDtypeStruct((64, 512), F32),
        ),
        in_specs=[smem, smem] + [vmem] * 5,
        out_specs=(vmem, vmem, vmem),
        scratch_shapes=[
            pltpu.VMEM((16, 2, 256, 512), BF),
            pltpu.VMEM((16, 256, 256), BF),
            pltpu.VMEM((2, 256, 512), F32),
            pltpu.VMEM((2, 256, 512), BF),
            pltpu.VMEM((2, 256, 512), BF),
            pltpu.VMEM((4, 2, 256, 256), BF),
            pltpu.VMEM((4, 2, 256, 256), BF),
            pltpu.VMEM((4, 2, 256, 256), F32),
            pltpu.VMEM((4, 2, 64, 256), BF),
            pltpu.VMEM((4, 2, 64, 256), BF),
            pltpu.VMEM((4, 2, 2, 64, 256), BF),
            pltpu.VMEM((4, 2, 2, 64, 256), BF),
            pltpu.VMEM((3, 2, 64, 256), BF),
            pltpu.VMEM((3, 2, 64, 256), BF),
            dma((4,)), dma((4,)),
            dma((4, 4)), dma((4, 4)),
            dma((4,)), dma((4,)),
            dma((2, 3 * CUTS)), dma((2, 3 * CUTS)),
            dma((6, STEPS)), dma((6, STEPS)),
            dma((4,)), dma((4,)),
            dma((4, 2)), dma((4, 2)),
            dma((4, 2)), dma((4, 2)),
            dma((3,)), dma((3,)),
        ],
        compiler_params=pltpu.CompilerParams(
            collective_id=0, has_side_effects=True, vmem_limit_bytes=48 * 1024 * 1024
        ),
        cost_estimate=pl.CostEstimate(flops=5 * 10**9, bytes_accessed=2 * 10**6, transcendentals=131072),
        name="fused",
    )(enc_lengths, dec_lengths, enc_out, query, w_key, w_value, d_context)


def solution(mesh):
    in_specs = (
        P(("dp", "pipe"), "mp"),
        P("pipe", "dp", "mp"),
        P("pipe", "dp", "mp"),
        P("pipe", "dp", "mp"),
        P("pipe", "dp", "mp"),
        P("dp"),
        P("dp"),
    )
    out_specs = (P("pipe", "dp", "mp"), P("pipe", "dp", "mp"), P(("dp", "pipe"), "mp"))
    return jax.shard_map(body, mesh=mesh, in_specs=in_specs, out_specs=out_specs, check_vma=False)
```

```python
import jax
import jax.numpy as jnp
from jax import lax
from jax.experimental import pallas as pl
from jax.experimental.pallas import tpu as pltpu
from jax.sharding import PartitionSpec as P

HD = 256
NEG = -1e30
BF = jnp.bfloat16
F32 = jnp.float32
FIRST = (16, 32, 48, 64, 64, 32)
SECOND = (64, 64, 64, 64)
THIRD = (64, 64, 48, 32, 32, 16)
OWN = (64, 64, 64, 64)
DEPTH = 4
LAG = 1


def spans(stage, sizes):
    return [(stage, sum(sizes[:n]), size) for n, size in enumerate(sizes)]


Z = spans(0, FIRST) + spans(1, SECOND) + spans(2, THIRD)
UNITS = spans(-1, OWN) + Z
NZ, NO, NU = len(Z), len(OWN), len(UNITS)

NT = (((1,), (1,)), ((), ()))
NN = (((1,), (0,)), ((), ()))
TN = (((0,), (0,)), ((), ()))


def dot(a, b, dims):
    return lax.dot_general(a, b, dims, preferred_element_type=F32)


def kernel(
    enc_len, dec_len, enc_ref, q_ref, wk_ref, wv_ref, dc_ref,
    ctx_ref, gq_ref, ge_ref,
    w, e, acc, kv, grads, s0, r0, part, x1s, x1r, x2s, x2r, zs, zr,
    ez_s, ez_r, ex_s, ex_r, ec_s, ec_r, z_s, z_r, y_s, y_r,
    c_s, c_r, x1_s, x1_r, x2_s, x2_r, q_s, q_r, in_s, q_v, dc_v,
):
    dp, x, mp = lax.axis_index("dp"), lax.axis_index("pipe"), lax.axis_index("mp")
    y, zh = dp // 4, dp % 4
    zl, core = mp // 2, mp % 2
    up, down = ((y + 1) % 4) * 4 + zh, ((y + 3) % 4) * 4 + zh
    nxt, prv = y * 4 + (zh + 1) % 4, y * 4 + (zh + 3) % 4
    d_up, d_down = (up, x, mp), (down, x, mp)
    d_next, d_prev = (nxt, x, mp), (prv, x, mp)
    d_right, d_left = (dp, (x + 1) % 4, mp), (dp, (x + 3) % 4, mp)
    d_sib = (dp, x, zl * 2 + 1 - core)
    d_line = [(dp, x, ((zl + r) % 4) * 2 + core) for r in range(4)]

    def rc(src, dst, ssem, rsem, dev):
        return pltpu.make_async_remote_copy(
            src_ref=src, dst_ref=dst, send_sem=ssem, recv_sem=rsem,
            device_id=dev, device_id_type=pl.DeviceIdType.MESH,
        )

    barrier = pltpu.get_barrier_semaphore()
    partners = [d_up, d_down, d_next, d_prev, d_right, d_left, d_sib] + d_line[1:]
    for dev in partners:
        pl.semaphore_signal(barrier, inc=1, device_id=dev, device_id_type=pl.DeviceIdType.MESH)

    my_rows = pl.ds(pl.multiple_of(x * 64, 64), 64)
    loads = [
        pltpu.make_async_copy(wk_ref.at[0], w.at[dp, 0], in_s.at[0]),
        pltpu.make_async_copy(wv_ref.at[0], w.at[dp, 1], in_s.at[1]),
        pltpu.make_async_copy(enc_ref.at[:, pl.ds(0, 256)], e.at[2 * mp, my_rows, :], in_s.at[2]),
        pltpu.make_async_copy(enc_ref.at[:, pl.ds(256, 256)], e.at[2 * mp + 1, my_rows, :], in_s.at[3]),
        pltpu.make_async_copy(q_ref.at[0], q_v, in_s.at[4]),
        pltpu.make_async_copy(dc_ref.at[0], dc_v, in_s.at[5]),
    ]
    for copy in loads:
        copy.start()
    acc[...] = jnp.zeros_like(acc)
    for copy in loads[:4]:
        copy.wait()
    pl.semaphore_wait(barrier, len(partners))

    def eblock(xx, zz, cc):
        return e.at[pl.ds(zz * 4 + cc * 2, 2), pl.ds(pl.multiple_of(xx * 64, 64), 64), :]

    def ehalf(xx, zz, cc, part_of):
        return e.at[zz * 4 + cc * 2 + part_of, pl.ds(pl.multiple_of(xx * 64, 64), 64), :]

    def e_line(r):
        b = eblock(x, zl, core)
        return rc(b, b, ez_s.at[r], ez_r.at[r], d_line[r])

    def e_line_in(r):
        b = eblock(x, (zl + 4 - r) % 4, core)
        return rc(b, b, ez_s.at[r], ez_r.at[r], d_line[r])

    def chunk(yy, zz, j, first, rows):
        return w.at[yy * 4 + zz, j, pl.ds(first, rows), :]

    def z_copy(t, inbound):
        stage, first, rows = Z[t]
        away = stage // 2 + inbound
        out = []
        for stream in (0, 1):
            zz = (zh + 4 - away) % 4 if stream == 0 else (zh + away) % 4
            c = chunk(y, zz, (stage + stream) % 2, first, rows)
            out.append(rc(c, c, z_s.at[stream, t], z_r.at[stream, t], d_next if stream == 0 else d_prev))
        return out

    def y_direct(i, inbound):
        stage, first, rows = UNITS[i]
        zz = [(zh + n) % 4 for n in ((0, 0), (3, 1), (1, 3), (2, 2))[stage + 1]]
        out = []
        for j in (0, 1):
            for way in (0, 1):
                yy = y if not inbound else ((y + 3) % 4 if way == 0 else (y + 1) % 4)
                c = chunk(yy, zz[j], j, first, rows)
                n = j * 2 + way
                out.append(rc(c, c, y_s.at[n, i], y_r.at[n, i], d_up if way == 0 else d_down))
        return out

    def y_forward(i, inbound):
        stage, first, rows = UNITS[i]
        zz = [(zh + n) % 4 for n in ((0, 0), (3, 1), (1, 3), (2, 2))[stage + 1]]
        out = []
        for j in (0, 1):
            away = 1 + inbound
            yy = (y + 4 - away) % 4 if j == 0 else (y + away) % 4
            c = chunk(yy, zz[j], j, first, rows)
            out.append(rc(c, c, y_s.at[4 + j, i], y_r.at[4 + j, i], d_up if j == 0 else d_down))
        return out

    def start(copies):
        for c in copies:
            c.start()

    def received(copies):
        for c in copies:
            c.wait_recv()

    def sent(copies):
        for c in copies:
            c.wait_send()

    def loop(lo, hi, body):
        lax.fori_loop(lo, hi, lambda i, carry: (body(i), carry)[1], 0)

    def ex_direct(r, inbound):
        zz = (zl + 4 - r) % 4
        out = []
        for way in (0, 1):
            xx = x if not inbound else ((x + 3) % 4 if way == 0 else (x + 1) % 4)
            b = eblock(xx, zz, core)
            out.append(rc(b, b, ex_s.at[way, r], ex_r.at[way, r], d_right if way == 0 else d_left))
        return out

    def ex_forward(r, inbound):
        zz = (zl + 4 - r) % 4
        out = []
        for way in (0, 1):
            away = 1 + inbound
            xx = (x + 4 - away) % 4 if way == 0 else (x + away) % 4
            b = ehalf(xx, zz, core, way)
            out.append(rc(b, b, ex_s.at[2 + way, r], ex_r.at[2 + way, r], d_right if way == 0 else d_left))
        return out

    def ec_copy(r, inbound):
        cc = 1 - core if inbound else core
        b = e.at[pl.ds(((zl + 4 - r) % 4) * 4 + cc * 2, 2)]
        return rc(b, b, ec_s.at[r], ec_r.at[r], d_sib)

    def add_block(yy, zz):
        d = yy * 4 + zz
        rows = e[d]
        for j in (0, 1):
            acc[j] = acc[j] + dot(rows, w[d, j], NN)

    def own(k):
        add_block((y + k) % 4, zh)

    def neighbours(k):
        add_block((y + k) % 4, (zh + 1) % 4)
        add_block((y + k) % 4, (zh + 3) % 4)

    def far(k):
        add_block((y + k) % 4, (zh + 2) % 4)

    def enc_stage(n):
        if n == 0:
            for r in (1, 3, 2):
                e_line_in(r).wait_recv()
                start(ex_direct(r, 0))
        elif n == 1:
            for r in (0, 1, 3, 2):
                received(ex_direct(r, 1))
                start(ex_forward(r, 0))
        elif n == 2:
            for r in (0, 1, 3, 2):
                received(ex_forward(r, 1))
                ec_copy(r, 0).start()
        elif n == 3:
            for r in (0, 1, 3, 2):
                ec_copy(r, 1).wait_recv()

    for r in (2, 1, 3):
        e_line(r).start()
    start(ex_direct(0, 0))
    for t in range(DEPTH):
        start(z_copy(t, 0))
    for i in range(NO):
        start(y_direct(i, 0))
    stepped = 0

    def y_until(n):
        nonlocal stepped
        while stepped < n:
            received(y_direct(stepped, 1))
            start(y_forward(stepped, 0))
            stepped += 1

    late = 0

    def late_until(n):
        nonlocal late
        while late < n:
            received(y_forward(late, 1))
            late += 1

    for t in range(NZ):
        received(z_copy(t, 1))
        start(y_direct(NO + t, 0))
        sent(z_copy(t, 0))
        if t + DEPTH < NZ:
            start(z_copy(t + DEPTH, 0))
        y_until(min(NO + t - LAG, (NU * (t + 1)) // NZ))
        enc_stage(t - 1)
        if t == 9:
            late_until(NO)
            loop(0, 4, own)
    near = NO + len(FIRST) + len(SECOND)
    y_until(NU - 1)
    late_until(near)
    loop(0, 4, neighbours)
    y_until(NU)
    late_until(NU)
    loop(0, 4, far)

    for copy in loads[4:]:
        copy.wait()
    scale = HD ** -0.5
    kv[...] = acc[...].astype(BF)
    shape = (256, 256)
    visible = lax.broadcasted_iota(jnp.int32, shape, 1) < enc_len[0]
    live = lax.broadcasted_iota(jnp.int32, shape, 0) < dec_len[0]
    for h in (0, 1):
        cols = slice(h * HD, (h + 1) * HD)
        q = q_v[:, cols]
        key, value = kv[0, :, cols], kv[1, :, cols]
        masked = jnp.where(live, dc_v[:, cols].astype(F32), 0.0)
        masked16 = masked.astype(BF)
        scores = jnp.where(visible, dot(q, key, NT) * scale, NEG)
        powers = jnp.exp(scores - jnp.max(scores, axis=1, keepdims=True))
        attention = powers / jnp.sum(powers, axis=1, keepdims=True)
        rounded = attention.astype(BF)
        context = dot(rounded, value, NN).astype(BF)
        ctx_ref[0, :, cols] = context
        weights = dot(masked16, value, NT)
        inner = jnp.sum(masked * context.astype(F32), axis=1, keepdims=True)
        g = (attention * (weights - inner) * scale).astype(BF)
        gq_ref[0, :, cols] = dot(g, key, NN).astype(BF)
        grads[0, :, cols] = dot(g, q, TN).astype(BF)
        grads[1, :, cols] = dot(rounded, masked16, TN).astype(BF)

    def place(k):
        return (zl + 1 + k) % 4

    def enc_term(k, cc, half):
        d = place(k) * 4 + cc * 2 + half
        return dot(grads[0], w[d, 0], NT) + dot(grads[1], w[d, 1], NT)

    def c_copy(k):
        return rc(s0.at[k], r0.at[k], c_s.at[k], c_r.at[k], d_sib)

    def quarter(n):
        return pl.ds(pl.multiple_of(((x + n) % 4) * 64, 64), 64)

    def x1_copy(k):
        return [
            rc(x1s.at[k, way], x1r.at[k, way], x1_s.at[k, way], x1_r.at[k, way], dev)
            for way, dev in ((0, d_right), (1, d_left))
        ]

    def x2_copy(k):
        return [
            rc(x2s.at[k, way], x2r.at[k, way], x2_s.at[k, way], x2_r.at[k, way], dev)
            for way, dev in ((0, d_right), (1, d_left))
        ]

    def q_copy(k):
        return rc(zs.at[k], zr.at[k], q_s.at[k], q_r.at[k], d_line[k + 1])

    def to_sibling(k):
        for half in (0, 1):
            s0[k, half] = enc_term(k, 1 - core, half).astype(BF)
        c_copy(k).start()

    def mine(k):
        for half in (0, 1):
            part[k, half] = enc_term(k, core, half)
        c_copy(k).wait_recv()
        part[k] = part[k] + r0[k].astype(F32)
        for way in (0, 1):
            x1s[k, way] = part[k, way, quarter(2), :].astype(BF)
        start(x1_copy(k))

    def second(k):
        received(x1_copy(k))
        for way in (0, 1):
            away = quarter(1 + 2 * way)
            for half in (0, 1):
                term = part[k, half, away, :]
                if half == way:
                    term = term + x1r[k, way].astype(F32)
                x2s[k, way, half] = term.astype(BF)
        start(x2_copy(k))

    def third(k):
        received(x2_copy(k))
        total = part[k, :, quarter(0), :] + x2r[k, 0].astype(F32) + x2r[k, 1].astype(F32)
        part[k, :, quarter(0), :] = total

    loop(0, 4, to_sibling)
    loop(0, 4, mine)
    loop(0, 4, second)
    for k in range(3):
        third(k)
        zs[k] = part[k, :, quarter(0), :].astype(BF)
        q_copy(k).start()
    third(3)
    total = part[3, :, quarter(0), :]
    for k in range(3):
        q_copy(k).wait_recv()
        total = total + zr[k].astype(F32)
    ge_ref[:, :256] = total[0]
    ge_ref[:, 256:] = total[1]

    for r in range(1, 4):
        e_line(r).wait_send()
    for r in range(4):
        sent(ex_direct(r, 0))
        sent(ex_forward(r, 0))
        ec_copy(r, 0).wait_send()

    for i in range(NU):
        sent(y_direct(i, 0))
        sent(y_forward(i, 0))

    def rest(k):
        c_copy(k).wait_send()
        sent(x1_copy(k))
        sent(x2_copy(k))

    loop(0, 4, rest)
    for k in range(3):
        q_copy(k).wait_send()


def body(enc_out, query, w_key, w_value, d_context, enc_lengths, dec_lengths):
    vmem = pl.BlockSpec(memory_space=pltpu.VMEM)
    smem = pl.BlockSpec(memory_space=pltpu.SMEM)
    hbm = pl.BlockSpec(memory_space=pltpu.HBM)
    dma = pltpu.SemaphoreType.DMA
    return pl.pallas_call(
        kernel,
        out_shape=(
            jax.ShapeDtypeStruct((1, 256, 512), BF),
            jax.ShapeDtypeStruct((1, 256, 512), BF),
            jax.ShapeDtypeStruct((64, 512), F32),
        ),
        in_specs=[smem, smem] + [hbm] * 5,
        out_specs=(vmem, vmem, vmem),
        scratch_shapes=[
            pltpu.VMEM((16, 2, 256, 512), BF),
            pltpu.VMEM((16, 256, 256), BF),
            pltpu.VMEM((2, 256, 512), F32),
            pltpu.VMEM((2, 256, 512), BF),
            pltpu.VMEM((2, 256, 512), BF),
            pltpu.VMEM((4, 2, 256, 256), BF),
            pltpu.VMEM((4, 2, 256, 256), BF),
            pltpu.VMEM((4, 2, 256, 256), F32),
            pltpu.VMEM((4, 2, 64, 256), BF),
            pltpu.VMEM((4, 2, 64, 256), BF),
            pltpu.VMEM((4, 2, 2, 64, 256), BF),
            pltpu.VMEM((4, 2, 2, 64, 256), BF),
            pltpu.VMEM((3, 2, 64, 256), BF),
            pltpu.VMEM((3, 2, 64, 256), BF),
            dma((4,)), dma((4,)),
            dma((4, 4)), dma((4, 4)),
            dma((4,)), dma((4,)),
            dma((2, NZ)), dma((2, NZ)),
            dma((6, NU)), dma((6, NU)),
            dma((4,)), dma((4,)),
            dma((4, 2)), dma((4, 2)),
            dma((4, 2)), dma((4, 2)),
            dma((3,)), dma((3,)), dma((6,)),
            pltpu.VMEM((256, 512), BF),
            pltpu.VMEM((256, 512), BF),
        ],
        compiler_params=pltpu.CompilerParams(
            collective_id=0, has_side_effects=True, vmem_limit_bytes=64 * 1024 * 1024
        ),
        cost_estimate=pl.CostEstimate(flops=5 * 10**9, bytes_accessed=2 * 10**6, transcendentals=131072),
        name="fused",
    )(enc_lengths, dec_lengths, enc_out, query, w_key, w_value, d_context)


def solution(mesh):
    in_specs = (
        P(("dp", "pipe"), "mp"),
        P("pipe", "dp", "mp"),
        P("pipe", "dp", "mp"),
        P("pipe", "dp", "mp"),
        P("pipe", "dp", "mp"),
        P("dp"),
        P("dp"),
    )
    out_specs = (P("pipe", "dp", "mp"), P("pipe", "dp", "mp"), P(("dp", "pipe"), "mp"))
    return jax.shard_map(body, mesh=mesh, in_specs=in_specs, out_specs=out_specs, check_vma=False)
```

```python
import jax
import jax.numpy as jnp
from jax import lax
from jax.experimental import pallas as pl
from jax.experimental.pallas import tpu as pltpu
from jax.sharding import PartitionSpec as P

HD = 256
NEG = -1e30
BF = jnp.bfloat16
F32 = jnp.float32
HEAD0 = ((64,) * 4,) * 3
HEAD1 = ((64,) * 4,) * 3
OWN = (128, 128)
DEPTH = 6
LAG = 1
ENC = (1, 3, 5, 7)


def spans(head, stage, sizes):
    return [(head, stage, sum(sizes[:n]), size) for n, size in enumerate(sizes)]


Z = [m for h, sizes in enumerate((HEAD0, HEAD1)) for stage in range(3) for m in spans(h, stage, sizes[stage])]
UNITS = spans(0, -1, OWN) + spans(1, -1, OWN) + Z
NZ, NO, NU = len(Z), 2 * len(OWN), 2 * len(OWN) + len(Z)
NZ0 = sum(len(sizes) for sizes in HEAD0)
CUT_NEAR = len(HEAD0[0]) + len(HEAD0[1])


NT = (((1,), (1,)), ((), ()))
NN = (((1,), (0,)), ((), ()))
TN = (((0,), (0,)), ((), ()))


def dot(a, b, dims):
    return lax.dot_general(a, b, dims, preferred_element_type=F32)


def kernel(
    enc_len, dec_len, enc_ref, q_ref, wk_ref, wv_ref, dc_ref,
    ctx_ref, gq_ref, ge_ref,
    w, e, acc, grads, away, s0, r0, part, x1s, x1r, x2s, x2r, zs, zr,
    ez_s, ez_r, ex_s, ex_r, ec_s, ec_r, z_s, z_r, y_s, y_r,
    c_s, c_r, x1_s, x1_r, x2_s, x2_r, q_s, q_r, in_s, q_v, dc_v, cred,
):
    dp, x, mp = lax.axis_index("dp"), lax.axis_index("pipe"), lax.axis_index("mp")
    y, zh = dp // 4, dp % 4
    zl, core = mp // 2, mp % 2
    up, down = ((y + 1) % 4) * 4 + zh, ((y + 3) % 4) * 4 + zh
    nxt, prv = y * 4 + (zh + 1) % 4, y * 4 + (zh + 3) % 4
    d_up, d_down = (up, x, mp), (down, x, mp)
    d_next, d_prev = (nxt, x, mp), (prv, x, mp)
    d_right, d_left = (dp, (x + 1) % 4, mp), (dp, (x + 3) % 4, mp)
    d_sib = (dp, x, zl * 2 + 1 - core)
    d_line = [(dp, x, ((zl + r) % 4) * 2 + core) for r in range(4)]

    def rc(src, dst, ssem, rsem, dev):
        return pltpu.make_async_remote_copy(
            src_ref=src, dst_ref=dst, send_sem=ssem, recv_sem=rsem,
            device_id=dev, device_id_type=pl.DeviceIdType.MESH,
        )

    barrier = pltpu.get_barrier_semaphore()
    partners = [d_up, d_down, d_next, d_prev, d_right, d_left, d_sib] + d_line[1:]
    for dev in partners:
        pl.semaphore_signal(barrier, inc=1, device_id=dev, device_id_type=pl.DeviceIdType.MESH)

    my_rows = pl.ds(pl.multiple_of(x * 64, 64), 64)
    loads = [
        pltpu.make_async_copy(ref.at[0, :, pl.ds(h * HD, HD)], w.at[dp, h, j], in_s.at[4 + 2 * h + j])
        for h in (0, 1)
        for j, ref in ((0, wk_ref), (1, wv_ref))
    ] + [
        pltpu.make_async_copy(enc_ref.at[:, pl.ds(0, 256)], e.at[2 * mp, my_rows, :], in_s.at[0]),
        pltpu.make_async_copy(enc_ref.at[:, pl.ds(256, 256)], e.at[2 * mp + 1, my_rows, :], in_s.at[1]),
        pltpu.make_async_copy(q_ref.at[0], q_v, in_s.at[2]),
        pltpu.make_async_copy(dc_ref.at[0], dc_v, in_s.at[3]),
    ]
    for copy in loads:
        copy.start()
    acc[...] = jnp.zeros_like(acc)
    for copy in loads[:6]:
        copy.wait()
    pl.semaphore_wait(barrier, len(partners))

    def eblock(xx, zz, cc):
        return e.at[pl.ds(zz * 4 + cc * 2, 2), pl.ds(pl.multiple_of(xx * 64, 64), 64), :]

    def ehalf(xx, zz, cc, part_of):
        return e.at[zz * 4 + cc * 2 + part_of, pl.ds(pl.multiple_of(xx * 64, 64), 64), :]

    def e_line(r):
        b = eblock(x, zl, core)
        return rc(b, b, ez_s.at[r], ez_r.at[r], d_line[r])

    def e_line_in(r):
        b = eblock(x, (zl + 4 - r) % 4, core)
        return rc(b, b, ez_s.at[r], ez_r.at[r], d_line[r])

    def chunk(yy, zz, h, j, first, rows):
        return w.at[yy * 4 + zz, h, j, pl.ds(first, rows), :]

    def z_copy(t, inbound):
        h, stage, first, rows = Z[t]
        away = stage // 2 + inbound
        out = []
        for stream in (0, 1):
            zz = (zh + 4 - away) % 4 if stream == 0 else (zh + away) % 4
            c = chunk(y, zz, h, (stage + stream) % 2, first, rows)
            out.append(rc(c, c, z_s.at[stream, t], z_r.at[stream, t], d_next if stream == 0 else d_prev))
        return out

    def y_direct(i, inbound):
        h, stage, first, rows = UNITS[i]
        zz = [(zh + n) % 4 for n in ((0, 0), (3, 1), (1, 3), (2, 2))[stage + 1]]
        out = []
        for j in (0, 1):
            for way in (0, 1):
                yy = y if not inbound else ((y + 3) % 4 if way == 0 else (y + 1) % 4)
                c = chunk(yy, zz[j], h, j, first, rows)
                n = j * 2 + way
                out.append(rc(c, c, y_s.at[n, i], y_r.at[n, i], d_up if way == 0 else d_down))
        return out

    def y_forward(i, inbound):
        h, stage, first, rows = UNITS[i]
        zz = [(zh + n) % 4 for n in ((0, 0), (3, 1), (1, 3), (2, 2))[stage + 1]]
        out = []
        for j in (0, 1):
            away = 1 + inbound
            yy = (y + 4 - away) % 4 if j == 0 else (y + away) % 4
            c = chunk(yy, zz[j], h, j, first, rows)
            out.append(rc(c, c, y_s.at[4 + j, i], y_r.at[4 + j, i], d_up if j == 0 else d_down))
        return out

    def start(copies):
        for c in copies:
            c.start()

    def received(copies):
        for c in copies:
            c.wait_recv()

    def sent(copies):
        for c in copies:
            c.wait_send()

    def loop(lo, hi, body):
        lax.fori_loop(lo, hi, lambda i, carry: (body(i), carry)[1], 0)

    def ex_direct(r, inbound):
        zz = (zl + 4 - r) % 4
        out = []
        for way in (0, 1):
            xx = x if not inbound else ((x + 3) % 4 if way == 0 else (x + 1) % 4)
            b = eblock(xx, zz, core)
            out.append(rc(b, b, ex_s.at[way, r], ex_r.at[way, r], d_right if way == 0 else d_left))
        return out

    def ex_forward(r, inbound):
        zz = (zl + 4 - r) % 4
        out = []
        for way in (0, 1):
            away = 1 + inbound
            xx = (x + 4 - away) % 4 if way == 0 else (x + away) % 4
            b = ehalf(xx, zz, core, way)
            out.append(rc(b, b, ex_s.at[2 + way, r], ex_r.at[2 + way, r], d_right if way == 0 else d_left))
        return out

    def ec_copy(r, inbound):
        cc = 1 - core if inbound else core
        b = e.at[pl.ds(((zl + 4 - r) % 4) * 4 + cc * 2, 2)]
        return rc(b, b, ec_s.at[r], ec_r.at[r], d_sib)

    def add_block(h, yy, zz):
        d = yy * 4 + zz
        rows = e[d]
        for j in (0, 1):
            acc[h, j] = acc[h, j] + dot(rows, w[d, h, j], NN)

    def add_own(h):
        loop(0, 4, lambda k: add_block(h, (y + k) % 4, zh))

    def add_near(h):
        def step(k):
            add_block(h, (y + k) % 4, (zh + 1) % 4)
            add_block(h, (y + k) % 4, (zh + 3) % 4)

        loop(0, 4, step)

    def add_far(h):
        loop(0, 4, lambda k: add_block(h, (y + k) % 4, (zh + 2) % 4))

    def attend(h):
        scale = HD ** -0.5
        shape = (256, 256)
        visible = lax.broadcasted_iota(jnp.int32, shape, 1) < enc_len[0]
        live = lax.broadcasted_iota(jnp.int32, shape, 0) < dec_len[0]
        cols = slice(h * HD, (h + 1) * HD)
        q = q_v[:, cols]
        key, value = acc[h, 0].astype(BF), acc[h, 1].astype(BF)
        masked = jnp.where(live, dc_v[:, cols].astype(F32), 0.0)
        masked16 = masked.astype(BF)
        scores = jnp.where(visible, dot(q, key, NT) * scale, NEG)
        powers = jnp.exp(scores - jnp.max(scores, axis=1, keepdims=True))
        attention = powers / jnp.sum(powers, axis=1, keepdims=True)
        rounded = attention.astype(BF)
        context = dot(rounded, value, NN).astype(BF)
        weights = dot(masked16, value, NT)
        inner = jnp.sum(masked * context.astype(F32), axis=1, keepdims=True)
        g = (attention * (weights - inner) * scale).astype(BF)
        grads[h, 0] = dot(g, q, TN).astype(BF)
        grads[h, 1] = dot(rounded, masked16, TN).astype(BF)
        ctx_ref[0, :, cols] = context
        gq_ref[0, :, cols] = dot(g, key, NN).astype(BF)

    def place(k):
        return (zl + 1 + k) % 4

    def enc_term(h, k, cc, half):
        d = place(k) * 4 + cc * 2 + half
        return dot(grads[h, 0], w[d, h, 0], NT) + dot(grads[h, 1], w[d, h, 1], NT)

    def early_terms(other):
        def step(k):
            for half in (0, 1):
                if other:
                    away[k, half] = enc_term(0, k, 1 - core, half)
                else:
                    part[k, half] = enc_term(0, k, core, half)

        loop(0, 4, step)

    def enc_stage(n):
        if n == 0:
            for r in (1, 3, 2):
                e_line_in(r).wait_recv()
                start(ex_direct(r, 0))
        elif n == 1:
            for r in (0, 1, 3, 2):
                received(ex_direct(r, 1))
                start(ex_forward(r, 0))
        elif n == 2:
            for r in (0, 1, 3, 2):
                received(ex_forward(r, 1))
                ec_copy(r, 0).start()
        elif n == 3:
            for r in (0, 1, 3, 2):
                ec_copy(r, 1).wait_recv()

    for r in (2, 1, 3):
        e_line(r).start()
    start(ex_direct(0, 0))
    for t in range(DEPTH):
        start(z_copy(t, 0))
    for i in range(NO):
        start(y_direct(i, 0))
    stepped = 0

    def y_until(n):
        nonlocal stepped
        while stepped < n:
            received(y_direct(stepped, 1))
            start(y_forward(stepped, 0))
            stepped += 1

    late = 0

    def late_until(n):
        nonlocal late
        while late < n:
            received(y_forward(late, 1))
            late += 1

    for t in range(NZ):
        received(z_copy(t, 1))
        start(y_direct(NO + t, 0))
        sent(z_copy(t, 0))
        if t + DEPTH < NZ:
            for dev in d_line[1:]:
                pl.semaphore_signal(cred.at[t], inc=1, device_id=dev, device_id_type=pl.DeviceIdType.MESH)
            pl.semaphore_wait(cred.at[t], 3)
            start(z_copy(t + DEPTH, 0))
        y_until(min(NO + t - LAG, (NU * (t + 1)) // NZ))
        enc_stage(ENC.index(t) if t in ENC else -1)
        if t == NZ0 - 1:
            late_until(NO)
            add_own(0)
            add_own(1)
        if t == NZ0 + 1:
            late_until(NO + CUT_NEAR)
            add_near(0)
        if t == NZ0 + 2:
            late_until(NO + NZ0)
            add_far(0)
        if t == NZ0 + 4:
            for copy in loads[6:]:
                copy.wait()
            attend(0)
        if t == NZ0 + 6:
            early_terms(True)
        if t == NZ0 + 8:
            early_terms(False)
    y_until(NU - 1)
    late_until(NU - len(HEAD1[2]))
    add_near(1)
    y_until(NU)
    late_until(NU)
    add_far(1)
    attend(1)

    def c_copy(k):
        return rc(s0.at[k], r0.at[k], c_s.at[k], c_r.at[k], d_sib)

    def quarter(n):
        return pl.ds(pl.multiple_of(((x + n) % 4) * 64, 64), 64)

    def x1_copy(k):
        return [
            rc(x1s.at[k, way], x1r.at[k, way], x1_s.at[k, way], x1_r.at[k, way], dev)
            for way, dev in ((0, d_right), (1, d_left))
        ]

    def x2_copy(k):
        return [
            rc(x2s.at[k, way], x2r.at[k, way], x2_s.at[k, way], x2_r.at[k, way], dev)
            for way, dev in ((0, d_right), (1, d_left))
        ]

    def q_copy(k):
        return rc(zs.at[k], zr.at[k], q_s.at[k], q_r.at[k], d_line[k + 1])

    def to_sibling(k):
        for half in (0, 1):
            s0[k, half] = (away[k, half] + enc_term(1, k, 1 - core, half)).astype(BF)
        c_copy(k).start()

    def mine(k):
        for half in (0, 1):
            part[k, half] = part[k, half] + enc_term(1, k, core, half)
        c_copy(k).wait_recv()
        part[k] = part[k] + r0[k].astype(F32)
        for way in (0, 1):
            x1s[k, way] = part[k, way, quarter(2), :].astype(BF)
        start(x1_copy(k))

    def second(k):
        received(x1_copy(k))
        for way in (0, 1):
            other = quarter(1 + 2 * way)
            for half in (0, 1):
                term = part[k, half, other, :]
                if half == way:
                    term = term + x1r[k, way].astype(F32)
                x2s[k, way, half] = term.astype(BF)
        start(x2_copy(k))

    def third(k):
        received(x2_copy(k))
        total = part[k, :, quarter(0), :] + x2r[k, 0].astype(F32) + x2r[k, 1].astype(F32)
        part[k, :, quarter(0), :] = total

    to_sibling(0)
    loop(0, 3, lambda k: (to_sibling(k + 1), mine(k)))
    mine(3)
    loop(0, 4, second)
    for k in range(3):
        third(k)
        zs[k] = part[k, :, quarter(0), :].astype(BF)
        q_copy(k).start()
    third(3)
    total = part[3, :, quarter(0), :]
    for k in range(3):
        q_copy(k).wait_recv()
        total = total + zr[k].astype(F32)
    ge_ref[:, :256] = total[0]
    ge_ref[:, 256:] = total[1]

    for r in range(1, 4):
        e_line(r).wait_send()
    for r in range(4):
        sent(ex_direct(r, 0))
        sent(ex_forward(r, 0))
        ec_copy(r, 0).wait_send()

    for i in range(NU):
        sent(y_direct(i, 0))
        sent(y_forward(i, 0))

    def rest(k):
        c_copy(k).wait_send()
        sent(x1_copy(k))
        sent(x2_copy(k))

    loop(0, 4, rest)
    for k in range(3):
        q_copy(k).wait_send()


def body(enc_out, query, w_key, w_value, d_context, enc_lengths, dec_lengths):
    vmem = pl.BlockSpec(memory_space=pltpu.VMEM)
    smem = pl.BlockSpec(memory_space=pltpu.SMEM)
    hbm = pl.BlockSpec(memory_space=pltpu.HBM)
    dma = pltpu.SemaphoreType.DMA
    return pl.pallas_call(
        kernel,
        out_shape=(
            jax.ShapeDtypeStruct((1, 256, 512), BF),
            jax.ShapeDtypeStruct((1, 256, 512), BF),
            jax.ShapeDtypeStruct((64, 512), F32),
        ),
        in_specs=[smem, smem] + [hbm] * 5,
        out_specs=(vmem, vmem, vmem),
        scratch_shapes=[
            pltpu.VMEM((16, 2, 2, 256, 256), BF),
            pltpu.VMEM((16, 256, 256), BF),
            pltpu.VMEM((2, 2, 256, 256), F32),
            pltpu.VMEM((2, 2, 256, 256), BF),
            pltpu.VMEM((4, 2, 256, 256), F32),
            pltpu.VMEM((4, 2, 256, 256), BF),
            pltpu.VMEM((4, 2, 256, 256), BF),
            pltpu.VMEM((4, 2, 256, 256), F32),
            pltpu.VMEM((4, 2, 64, 256), BF),
            pltpu.VMEM((4, 2, 64, 256), BF),
            pltpu.VMEM((4, 2, 2, 64, 256), BF),
            pltpu.VMEM((4, 2, 2, 64, 256), BF),
            pltpu.VMEM((3, 2, 64, 256), BF),
            pltpu.VMEM((3, 2, 64, 256), BF),
            dma((4,)), dma((4,)),
            dma((4, 4)), dma((4, 4)),
            dma((4,)), dma((4,)),
            dma((2, NZ)), dma((2, NZ)),
            dma((6, NU)), dma((6, NU)),
            dma((4,)), dma((4,)),
            dma((4, 2)), dma((4, 2)),
            dma((4, 2)), dma((4, 2)),
            dma((3,)), dma((3,)), dma((8,)),
            pltpu.VMEM((256, 512), BF),
            pltpu.VMEM((256, 512), BF),
            pltpu.SemaphoreType.REGULAR((NZ,)),
        ],
        compiler_params=pltpu.CompilerParams(
            collective_id=0, has_side_effects=True, vmem_limit_bytes=55836672
        ),
        cost_estimate=pl.CostEstimate(flops=5 * 10**9, bytes_accessed=2 * 10**6, transcendentals=131072),
        name="fused",
    )(enc_lengths, dec_lengths, enc_out, query, w_key, w_value, d_context)


def solution(mesh):
    in_specs = (
        P(("dp", "pipe"), "mp"),
        P("pipe", "dp", "mp"),
        P("pipe", "dp", "mp"),
        P("pipe", "dp", "mp"),
        P("pipe", "dp", "mp"),
        P("dp"),
        P("dp"),
    )
    out_specs = (P("pipe", "dp", "mp"), P("pipe", "dp", "mp"), P(("dp", "pipe"), "mp"))
    return jax.shard_map(body, mesh=mesh, in_specs=in_specs, out_specs=out_specs, check_vma=False)
```

```python
import jax
import jax.numpy as jnp
from jax import lax
from jax.experimental import pallas as pl
from jax.experimental.pallas import tpu as pltpu
from jax.sharding import PartitionSpec as P

HD = 256
NEG = -1e30
BF = jnp.bfloat16
F32 = jnp.float32
HEAD0 = ((64,) * 4,) * 3
HEAD1 = ((64,) * 4,) * 3
OWN = (128, 128)
DEPTH = 6
LAG = 1
ENC = (1, 3, 5, 7)


def spans(head, stage, sizes):
    return [(head, stage, sum(sizes[:n]), size) for n, size in enumerate(sizes)]


Z = [m for h, sizes in enumerate((HEAD0, HEAD1)) for stage in range(3) for m in spans(h, stage, sizes[stage])]
UNITS = spans(0, -1, OWN) + spans(1, -1, OWN) + Z
NZ, NO, NU = len(Z), 2 * len(OWN), 2 * len(OWN) + len(Z)
NZ0 = sum(len(sizes) for sizes in HEAD0)
CUT_NEAR = len(HEAD0[0]) + len(HEAD0[1])


NT = (((1,), (1,)), ((), ()))
NN = (((1,), (0,)), ((), ()))
TN = (((0,), (0,)), ((), ()))


def dot(a, b, dims):
    return lax.dot_general(a, b, dims, preferred_element_type=F32)


def kernel(
    enc_len, dec_len, enc_ref, q_ref, wk_ref, wv_ref, dc_ref,
    ctx_ref, gq_ref, ge_ref,
    w, e, acc, grads, away, s0, r0, part, x1s, x1r, x2s, x2r, zs, zr,
    ez_s, ez_r, ex_s, ex_r, ec_s, ec_r, z_s, z_r, y_s, y_r,
    c_s, c_r, x1_s, x1_r, x2_s, x2_r, q_s, q_r, in_s, q_v, dc_v, cred,
):
    dp, x, mp = lax.axis_index("dp"), lax.axis_index("pipe"), lax.axis_index("mp")
    y, zh = dp // 4, dp % 4
    zl, core = mp // 2, mp % 2
    up, down = ((y + 1) % 4) * 4 + zh, ((y + 3) % 4) * 4 + zh
    nxt, prv = y * 4 + (zh + 1) % 4, y * 4 + (zh + 3) % 4
    d_up, d_down = (up, x, mp), (down, x, mp)
    d_next, d_prev = (nxt, x, mp), (prv, x, mp)
    d_right, d_left = (dp, (x + 1) % 4, mp), (dp, (x + 3) % 4, mp)
    d_sib = (dp, x, zl * 2 + 1 - core)
    d_line = [(dp, x, ((zl + r) % 4) * 2 + core) for r in range(4)]

    def rc(src, dst, ssem, rsem, dev):
        return pltpu.make_async_remote_copy(
            src_ref=src, dst_ref=dst, send_sem=ssem, recv_sem=rsem,
            device_id=dev, device_id_type=pl.DeviceIdType.MESH,
        )

    barrier = pltpu.get_barrier_semaphore()
    partners = [d_up, d_down, d_next, d_prev, d_right, d_left, d_sib] + d_line[1:]
    for dev in partners:
        pl.semaphore_signal(barrier, inc=1, device_id=dev, device_id_type=pl.DeviceIdType.MESH)

    my_rows = pl.ds(pl.multiple_of(x * 64, 64), 64)
    loads = [
        pltpu.make_async_copy(ref.at[0, :, pl.ds(h * HD, HD)], w.at[dp, h, j], in_s.at[4 + 2 * h + j])
        for h in (0, 1)
        for j, ref in ((0, wk_ref), (1, wv_ref))
    ] + [
        pltpu.make_async_copy(enc_ref.at[:, pl.ds(0, 256)], e.at[2 * mp, my_rows, :], in_s.at[0]),
        pltpu.make_async_copy(enc_ref.at[:, pl.ds(256, 256)], e.at[2 * mp + 1, my_rows, :], in_s.at[1]),
        pltpu.make_async_copy(q_ref.at[0], q_v, in_s.at[2]),
        pltpu.make_async_copy(dc_ref.at[0], dc_v, in_s.at[3]),
    ]
    for copy in loads:
        copy.start()
    acc[...] = jnp.zeros_like(acc)
    for copy in loads[:6]:
        copy.wait()
    pl.semaphore_wait(barrier, len(partners))

    def eblock(xx, zz, cc):
        return e.at[pl.ds(zz * 4 + cc * 2, 2), pl.ds(pl.multiple_of(xx * 64, 64), 64), :]

    def ehalf(xx, zz, cc, part_of):
        return e.at[zz * 4 + cc * 2 + part_of, pl.ds(pl.multiple_of(xx * 64, 64), 64), :]

    def e_line(r):
        b = eblock(x, zl, core)
        return rc(b, b, ez_s.at[r], ez_r.at[r], d_line[r])

    def e_line_in(r):
        b = eblock(x, (zl + 4 - r) % 4, core)
        return rc(b, b, ez_s.at[r], ez_r.at[r], d_line[r])

    def chunk(yy, zz, h, j, first, rows):
        return w.at[yy * 4 + zz, h, j, pl.ds(first, rows), :]

    def z_copy(t, inbound):
        h, stage, first, rows = Z[t]
        away = stage // 2 + inbound
        out = []
        for stream in (0, 1):
            zz = (zh + 4 - away) % 4 if stream == 0 else (zh + away) % 4
            c = chunk(y, zz, h, (stage + stream) % 2, first, rows)
            out.append(rc(c, c, z_s.at[stream, t], z_r.at[stream, t], d_next if stream == 0 else d_prev))
        return out

    def y_direct(i, inbound):
        h, stage, first, rows = UNITS[i]
        zz = [(zh + n) % 4 for n in ((0, 0), (3, 1), (1, 3), (2, 2))[stage + 1]]
        out = []
        for j in (0, 1):
            for way in (0, 1):
                yy = y if not inbound else ((y + 3) % 4 if way == 0 else (y + 1) % 4)
                c = chunk(yy, zz[j], h, j, first, rows)
                n = j * 2 + way
                out.append(rc(c, c, y_s.at[n, i], y_r.at[n, i], d_up if way == 0 else d_down))
        return out

    def y_forward(i, inbound):
        h, stage, first, rows = UNITS[i]
        zz = [(zh + n) % 4 for n in ((0, 0), (3, 1), (1, 3), (2, 2))[stage + 1]]
        out = []
        for j in (0, 1):
            away = 1 + inbound
            yy = (y + 4 - away) % 4 if j == 0 else (y + away) % 4
            c = chunk(yy, zz[j], h, j, first, rows)
            out.append(rc(c, c, y_s.at[4 + j, i], y_r.at[4 + j, i], d_up if j == 0 else d_down))
        return out

    def start(copies):
        for c in copies:
            c.start()

    def received(copies):
        for c in copies:
            c.wait_recv()

    def sent(copies):
        for c in copies:
            c.wait_send()

    def loop(lo, hi, body):
        lax.fori_loop(lo, hi, lambda i, carry: (body(i), carry)[1], 0)

    def ex_direct(r, inbound):
        zz = (zl + 4 - r) % 4
        out = []
        for way in (0, 1):
            xx = x if not inbound else ((x + 3) % 4 if way == 0 else (x + 1) % 4)
            b = eblock(xx, zz, core)
            out.append(rc(b, b, ex_s.at[way, r], ex_r.at[way, r], d_right if way == 0 else d_left))
        return out

    def ex_forward(r, inbound):
        zz = (zl + 4 - r) % 4
        out = []
        for way in (0, 1):
            away = 1 + inbound
            xx = (x + 4 - away) % 4 if way == 0 else (x + away) % 4
            b = ehalf(xx, zz, core, way)
            out.append(rc(b, b, ex_s.at[2 + way, r], ex_r.at[2 + way, r], d_right if way == 0 else d_left))
        return out

    def ec_copy(r, inbound):
        cc = 1 - core if inbound else core
        b = e.at[pl.ds(((zl + 4 - r) % 4) * 4 + cc * 2, 2)]
        return rc(b, b, ec_s.at[r], ec_r.at[r], d_sib)

    def add_block(h, yy, zz):
        d = yy * 4 + zz
        rows = e[d]
        for j in (0, 1):
            acc[h, j] = acc[h, j] + dot(rows, w[d, h, j], NN)

    def add_own(h):
        loop(0, 4, lambda k: add_block(h, (y + k) % 4, zh))

    def add_near(h):
        def step(k):
            add_block(h, (y + k) % 4, (zh + 1) % 4)
            add_block(h, (y + k) % 4, (zh + 3) % 4)

        loop(0, 4, step)

    def add_far(h):
        loop(0, 4, lambda k: add_block(h, (y + k) % 4, (zh + 2) % 4))

    def attend(h):
        scale = HD ** -0.5
        shape = (256, 256)
        visible = lax.broadcasted_iota(jnp.int32, shape, 1) < enc_len[0]
        live = lax.broadcasted_iota(jnp.int32, shape, 0) < dec_len[0]
        cols = slice(h * HD, (h + 1) * HD)
        q = q_v[:, cols]
        key, value = acc[h, 0].astype(BF), acc[h, 1].astype(BF)
        masked = jnp.where(live, dc_v[:, cols].astype(F32), 0.0)
        masked16 = masked.astype(BF)
        scores = jnp.where(visible, dot(q, key, NT) * scale, NEG)
        powers = jnp.exp(scores - jnp.max(scores, axis=1, keepdims=True))
        attention = powers / jnp.sum(powers, axis=1, keepdims=True)
        rounded = attention.astype(BF)
        context = dot(rounded, value, NN).astype(BF)
        weights = dot(masked16, value, NT)
        inner = jnp.sum(masked * context.astype(F32), axis=1, keepdims=True)
        g = (attention * (weights - inner) * scale).astype(BF)
        grads[h, 0] = dot(g, q, TN).astype(BF)
        grads[h, 1] = dot(rounded, masked16, TN).astype(BF)
        ctx_ref[0, :, cols] = context
        gq_ref[0, :, cols] = dot(g, key, NN).astype(BF)

    def place(k):
        return (zl + 1 + k) % 4

    def enc_term(h, k, cc, half):
        d = place(k) * 4 + cc * 2 + half
        return dot(grads[h, 0], w[d, h, 0], NT) + dot(grads[h, 1], w[d, h, 1], NT)

    def early_terms(other):
        def step(k):
            for half in (0, 1):
                if other:
                    away[k, half] = enc_term(0, k, 1 - core, half)
                else:
                    part[k, half] = enc_term(0, k, core, half)

        loop(0, 4, step)

    def enc_stage(n):
        if n == 0:
            for r in (1, 3, 2):
                e_line_in(r).wait_recv()
                start(ex_direct(r, 0))
        elif n == 1:
            for r in (0, 1, 3, 2):
                received(ex_direct(r, 1))
                start(ex_forward(r, 0))
        elif n == 2:
            for r in (0, 1, 3, 2):
                received(ex_forward(r, 1))
                ec_copy(r, 0).start()
        elif n == 3:
            for r in (0, 1, 3, 2):
                ec_copy(r, 1).wait_recv()

    for r in (2, 1, 3):
        e_line(r).start()
    start(ex_direct(0, 0))
    for t in range(DEPTH):
        start(z_copy(t, 0))
    for i in range(NO):
        start(y_direct(i, 0))
    stepped = 0

    def y_until(n):
        nonlocal stepped
        while stepped < n:
            received(y_direct(stepped, 1))
            start(y_forward(stepped, 0))
            stepped += 1

    late = 0

    def late_until(n):
        nonlocal late
        while late < n:
            received(y_forward(late, 1))
            late += 1

    for t in range(NZ):
        received(z_copy(t, 1))
        start(y_direct(NO + t, 0))
        sent(z_copy(t, 0))
        if t + DEPTH < NZ:
            for dev in d_line[1:]:
                pl.semaphore_signal(cred.at[t], inc=1, device_id=dev, device_id_type=pl.DeviceIdType.MESH)
            pl.semaphore_wait(cred.at[t], 3)
            start(z_copy(t + DEPTH, 0))
        y_until(min(NO + t - LAG, (NU * (t + 1)) // NZ))
        enc_stage(ENC.index(t) if t in ENC else -1)
        if t == NZ0 - 1:
            late_until(NO)
            add_own(0)
            add_own(1)
        if t == NZ0 + 1:
            late_until(NO + CUT_NEAR)
            add_near(0)
        if t == NZ0 + 2:
            late_until(NO + NZ0)
            add_far(0)
        if t == NZ0 + 4:
            for copy in loads[6:]:
                copy.wait()
            attend(0)
        if t == NZ0 + 6:
            early_terms(True)
        if t == NZ0 + 8:
            early_terms(False)
    y_until(NU - 1)
    late_until(NU - len(HEAD1[2]))
    add_near(1)
    y_until(NU)
    for k in (0, 1, 3):
        add_block(1, (y + k) % 4, (zh + 2) % 4)
    late_until(NU)
    add_block(1, (y + 2) % 4, (zh + 2) % 4)
    attend(1)

    def c_copy(k):
        return rc(s0.at[k], r0.at[k], c_s.at[k], c_r.at[k], d_sib)

    def quarter(n):
        return pl.ds(pl.multiple_of(((x + n) % 4) * 64, 64), 64)

    def x1_copy(k):
        return [
            rc(x1s.at[k, way], x1r.at[k, way], x1_s.at[k, way], x1_r.at[k, way], dev)
            for way, dev in ((0, d_right), (1, d_left))
        ]

    def x2_copy(k):
        return [
            rc(x2s.at[k, way], x2r.at[k, way], x2_s.at[k, way], x2_r.at[k, way], dev)
            for way, dev in ((0, d_right), (1, d_left))
        ]

    def q_copy(k):
        return rc(zs.at[k], zr.at[k], q_s.at[k], q_r.at[k], d_line[k + 1])

    def to_sibling(k):
        for half in (0, 1):
            s0[k, half] = (away[k, half] + enc_term(1, k, 1 - core, half)).astype(BF)
        c_copy(k).start()

    def mine(k):
        for half in (0, 1):
            part[k, half] = part[k, half] + enc_term(1, k, core, half)
        c_copy(k).wait_recv()
        part[k] = part[k] + r0[k].astype(F32)
        for way in (0, 1):
            x1s[k, way] = part[k, way, quarter(2), :].astype(BF)
        start(x1_copy(k))

    def second(k):
        received(x1_copy(k))
        for way in (0, 1):
            other = quarter(1 + 2 * way)
            for half in (0, 1):
                term = part[k, half, other, :]
                if half == way:
                    term = term + x1r[k, way].astype(F32)
                x2s[k, way, half] = term.astype(BF)
        start(x2_copy(k))

    def third(k):
        received(x2_copy(k))
        total = part[k, :, quarter(0), :] + x2r[k, 0].astype(F32) + x2r[k, 1].astype(F32)
        part[k, :, quarter(0), :] = total

    to_sibling(0)
    loop(0, 3, lambda k: (to_sibling(k + 1), mine(k)))
    mine(3)
    loop(0, 4, second)
    for k in range(3):
        third(k)
        zs[k] = part[k, :, quarter(0), :].astype(BF)
        q_copy(k).start()
    third(3)
    total = part[3, :, quarter(0), :]
    for k in range(3):
        q_copy(k).wait_recv()
        total = total + zr[k].astype(F32)
    ge_ref[:, :256] = total[0]
    ge_ref[:, 256:] = total[1]

    for r in range(1, 4):
        e_line(r).wait_send()
    for r in range(4):
        sent(ex_direct(r, 0))
        sent(ex_forward(r, 0))
        ec_copy(r, 0).wait_send()

    for i in range(NU):
        sent(y_direct(i, 0))
        sent(y_forward(i, 0))

    def rest(k):
        c_copy(k).wait_send()
        sent(x1_copy(k))
        sent(x2_copy(k))

    loop(0, 4, rest)
    for k in range(3):
        q_copy(k).wait_send()


def body(enc_out, query, w_key, w_value, d_context, enc_lengths, dec_lengths):
    vmem = pl.BlockSpec(memory_space=pltpu.VMEM)
    smem = pl.BlockSpec(memory_space=pltpu.SMEM)
    hbm = pl.BlockSpec(memory_space=pltpu.HBM)
    dma = pltpu.SemaphoreType.DMA
    return pl.pallas_call(
        kernel,
        out_shape=(
            jax.ShapeDtypeStruct((1, 256, 512), BF),
            jax.ShapeDtypeStruct((1, 256, 512), BF),
            jax.ShapeDtypeStruct((64, 512), F32),
        ),
        in_specs=[smem, smem] + [hbm] * 5,
        out_specs=(vmem, vmem, vmem),
        scratch_shapes=[
            pltpu.VMEM((16, 2, 2, 256, 256), BF),
            pltpu.VMEM((16, 256, 256), BF),
            pltpu.VMEM((2, 2, 256, 256), F32),
            pltpu.VMEM((2, 2, 256, 256), BF),
            pltpu.VMEM((4, 2, 256, 256), F32),
            pltpu.VMEM((4, 2, 256, 256), BF),
            pltpu.VMEM((4, 2, 256, 256), BF),
            pltpu.VMEM((4, 2, 256, 256), F32),
            pltpu.VMEM((4, 2, 64, 256), BF),
            pltpu.VMEM((4, 2, 64, 256), BF),
            pltpu.VMEM((4, 2, 2, 64, 256), BF),
            pltpu.VMEM((4, 2, 2, 64, 256), BF),
            pltpu.VMEM((3, 2, 64, 256), BF),
            pltpu.VMEM((3, 2, 64, 256), BF),
            dma((4,)), dma((4,)),
            dma((4, 4)), dma((4, 4)),
            dma((4,)), dma((4,)),
            dma((2, NZ)), dma((2, NZ)),
            dma((6, NU)), dma((6, NU)),
            dma((4,)), dma((4,)),
            dma((4, 2)), dma((4, 2)),
            dma((4, 2)), dma((4, 2)),
            dma((3,)), dma((3,)), dma((8,)),
            pltpu.VMEM((256, 512), BF),
            pltpu.VMEM((256, 512), BF),
            pltpu.SemaphoreType.REGULAR((NZ,)),
        ],
        compiler_params=pltpu.CompilerParams(
            collective_id=0, has_side_effects=True, vmem_limit_bytes=55836672
        ),
        cost_estimate=pl.CostEstimate(flops=5 * 10**9, bytes_accessed=2 * 10**6, transcendentals=131072),
        name="fused",
    )(enc_lengths, dec_lengths, enc_out, query, w_key, w_value, d_context)


def solution(mesh):
    in_specs = (
        P(("dp", "pipe"), "mp"),
        P("pipe", "dp", "mp"),
        P("pipe", "dp", "mp"),
        P("pipe", "dp", "mp"),
        P("pipe", "dp", "mp"),
        P("dp"),
        P("dp"),
    )
    out_specs = (P("pipe", "dp", "mp"), P("pipe", "dp", "mp"), P(("dp", "pipe"), "mp"))
    return jax.shard_map(body, mesh=mesh, in_specs=in_specs, out_specs=out_specs, check_vma=False)
```
